32 devices in a mesh: grp: 2 (over x), sa: 16 (over z, y, core).
Axes of the slice: x: 2, y: 2, z: 4, core: 2. Of those that a mesh axis runs over, the one named last changes fastest.
Arguments:
- tokens: float32 [16384, 768], P(('grp', 'sa')), parts along dimension 0, may hold values from -6 to 6
- kernel_re: float32 [16384, 768], P(('grp', 'sa')), parts along dimension 0, may hold values from -6 to 6
- kernel_im: float32 [16384, 768], P(('grp', 'sa')), parts along dimension 0, may hold values from -6 to 6
- mix_gain: float32 [768], replicated, may hold values from 0.1 to 1.9
- mlp_gain: float32 [768], replicated, may hold values from 0.1 to 1.9
- w_in: bfloat16 [768, 3072], P('sa'), may hold values from -0.21875 to 0.21875
- w_out: bfloat16 [3072, 768], P('sa'), may hold values from -0.109375 to 0.109375
Outputs:
- layer_out: float32 [16384, 768], P(('grp', 'sa')), parts along dimension 0
The draws below stay inside these ranges and needn't reach their ends.
There are 2 independent parts, one for each index of `grp`. The reference program is written for one: setup_inputs(seed, part) draws one part's arguments, and reference() takes and returns one part's arrays. A program takes and returns all parts, laid end to end along the dimension named above; an argument that names none is the same for every part. Nothing has to cross between parts.
All inputs are finite; a program needn't handle non-finite values.
Results may differ from the reference program's by a relative error of at most 0.0022.
Values may be sent and summed in bfloat16 or wider, within the bound.
A program may use at most 128 MiB of HBM per device.

```python
import jax
import jax.numpy as jnp
from jax import lax

D = 768
FF = 3072
SEQ = 8192


def level_of(stream_key, extent, split, smallest, largest):
    loudness = 1.0
    for dim, blocks in split:
        heights = jax.random.uniform(jax.random.fold_in(jax.random.fold_in(stream_key, 6), dim), (blocks,), jnp.float32, smallest / len(split), largest / len(split))
        loudness = loudness * jnp.repeat(jnp.exp(heights), extent[dim] // blocks).reshape((-1,) + (1,) * (len(extent) - 1 - dim))
    return loudness


def normal_values(own_key, dims, spread, most, shards=(), dtype=jnp.bfloat16):
    drawn = spread * jax.random.normal(own_key, dims, jnp.float32)
    if shards:
        drawn = drawn * level_of(own_key, dims, shards, -0.22, 0.18)
    return jnp.clip(drawn, -most, most).astype(dtype)


def setup_inputs(seed: int = 0, part: int = 0) -> dict:
    key_of = jax.random.split(jax.random.key(seed), 8)
    part_keys = jax.random.split(jax.random.fold_in(key_of[7], part), 8)
    tokens = normal_values(part_keys[0], (SEQ, D), 1.0, 6.0, ((0, 16),), jnp.float32)
    kernel_re = normal_values(part_keys[1], (SEQ, D), 1.0, 6.0, ((0, 16),), jnp.float32)
    kernel_im = normal_values(part_keys[2], (SEQ, D), 1.0, 6.0, ((0, 16),), jnp.float32)
    mix_gain = jnp.clip(1.0 + 0.18 * jax.random.normal(key_of[3], (D,), jnp.float32), 0.1, 1.9)
    mlp_gain = jnp.clip(1.0 + 0.18 * jax.random.normal(key_of[4], (D,), jnp.float32), 0.1, 1.9)
    w_in = normal_values(key_of[5], (D, FF), D ** -0.5, 0.21875, ((0, 16),))
    w_out = normal_values(key_of[6], (FF, D), FF ** -0.5, 0.109375, ((0, 16),))
    return {"tokens": tokens, "kernel_re": kernel_re, "kernel_im": kernel_im, "mix_gain": mix_gain, "mlp_gain": mlp_gain, "w_in": w_in, "w_out": w_out}


def rms_scale(values):
    return values * lax.rsqrt(lax.optimization_barrier(jnp.mean(values * values, axis=-1, keepdims=True)) + 1e-06)

def filter_channel(columns):
    signal, real_kernel, imag_kernel = columns
    spectrum = jnp.fft.fft(signal)
    return jnp.real(jnp.fft.ifft(spectrum * lax.complex(real_kernel, imag_kernel)))

def reference(tokens, kernel_re, kernel_im, mix_gain, mlp_gain, w_in, w_out):
    normed = rms_scale(tokens) * mix_gain
    conv = lax.map(filter_channel, (normed.T, kernel_re.T, kernel_im.T)).T
    mixed = tokens + conv * jax.nn.sigmoid(normed)
    scaled = (rms_scale(mixed) * mlp_gain).astype(jnp.bfloat16)
    hidden_pre = jnp.dot(scaled, w_in, preferred_element_type=jnp.float32)
    hidden = jax.nn.gelu(hidden_pre, approximate=True).astype(jnp.bfloat16)
    return mixed + jnp.dot(hidden, w_out, preferred_element_type=jnp.float32)
```

```python
import jax
import jax.numpy as jnp
import numpy as np
from jax import lax
from jax.sharding import PartitionSpec as P

LANES = 128
EPSILON = 1e-06
LINK = jnp.float16
CONV_SCALE = 0.125


def rms_scale(values):
    return values * lax.rsqrt(jnp.mean(values * values, axis=-1, keepdims=True) + EPSILON)


def angles(first, second, period):
    product = np.outer(np.arange(first, dtype=np.int64), np.arange(second, dtype=np.int64)) % period
    phase = product.astype(np.float64) * (2 * np.pi / period)
    return np.cos(phase), np.sin(phase)


def contract(pattern, left, right):
    return jnp.einsum(
        pattern, left, right, precision=lax.Precision.HIGH, preferred_element_type=jnp.float32
    )


def on_device(tokens, kernel_re, kernel_im, mix_gain, mlp_gain, w_in, w_out):
    shards = lax.axis_size("sa")
    rows, channels = tokens.shape
    part = channels // shards
    blocks = rows // LANES
    total = shards * rows
    outer = total // LANES

    def to_channels(values):
        packed = values.astype(LINK).reshape(blocks, LANES, shards, part).transpose(2, 0, 3, 1)
        moved = lax.all_to_all(packed, "sa", split_axis=0, concat_axis=0, tiled=True)
        return moved.reshape(outer, part, LANES)

    normed = rms_scale(tokens) * mix_gain
    signal = to_channels(normed).astype(jnp.float32)

    def by_frequency(moved):
        ordered = moved.transpose(1, 0, 2).reshape(part, LANES, outer)
        return ordered.transpose(2, 0, 1).astype(jnp.float32)

    filter_re = by_frequency(to_channels(kernel_re))
    filter_im = by_frequency(to_channels(kernel_im))

    cos_outer, sin_outer = angles(outer, outer, outer)
    cos_inner, sin_inner = angles(LANES, LANES, LANES)
    cos_twist, sin_twist = angles(outer, LANES, total)
    first = jnp.asarray(np.concatenate([cos_outer, -sin_outer], 0), jnp.float32)
    last = jnp.asarray(np.concatenate([cos_outer, -sin_outer], 1), jnp.float32)
    forward = jnp.asarray(
        np.block([[cos_inner, -sin_inner], [sin_inner, cos_inner]]), jnp.float32
    )
    backward = jnp.asarray(
        np.block([[cos_inner, sin_inner], [-sin_inner, cos_inner]]), jnp.float32
    )
    cos_twist = jnp.asarray(cos_twist[:, None, :], jnp.float32)
    sin_twist = jnp.asarray(sin_twist[:, None, :], jnp.float32)

    mid = contract("ca,adb->cdb", first, signal)
    mid_re, mid_im = mid[:outer], mid[outer:]
    turned = jnp.concatenate(
        [mid_re * cos_twist + mid_im * sin_twist, mid_im * cos_twist - mid_re * sin_twist], -1
    )
    spectrum = contract("cdb,be->cde", turned, forward)
    spec_re, spec_im = spectrum[..., :LANES], spectrum[..., LANES:]
    filtered = jnp.concatenate(
        [spec_re * filter_re - spec_im * filter_im, spec_re * filter_im + spec_im * filter_re], -1
    )
    back = contract("cde,eb->cdb", filtered, backward)
    back_re, back_im = back[..., :LANES], back[..., LANES:]
    untwisted = jnp.concatenate(
        [back_re * cos_twist - back_im * sin_twist, back_im * cos_twist + back_re * sin_twist], 0
    )
    conv = contract("ac,cdb->adb", last, untwisted)
    conv = (conv * (CONV_SCALE / total)).astype(LINK).reshape(shards, blocks, part, LANES)
    conv = lax.all_to_all(conv, "sa", split_axis=0, concat_axis=0, tiled=True)
    conv = conv.transpose(1, 3, 0, 2).reshape(rows, channels).astype(jnp.float32) * (1 / CONV_SCALE)

    mixed = tokens + conv * jax.nn.sigmoid(normed)
    scaled = (rms_scale(mixed) * mlp_gain).astype(jnp.bfloat16)
    hidden_pre = jnp.dot(
        scaled, lax.all_gather(w_in, "sa", axis=0, tiled=True), preferred_element_type=jnp.float32
    )
    hidden = jax.nn.gelu(hidden_pre, approximate=True).astype(jnp.bfloat16)
    branch = jnp.dot(
        hidden, lax.all_gather(w_out, "sa", axis=0, tiled=True), preferred_element_type=jnp.float32
    )
    return mixed + branch


def solution(mesh):
    return jax.shard_map(
        on_device,
        mesh=mesh,
        in_specs=(
            P(("grp", "sa"), None),
            P(("grp", "sa"), None),
            P(("grp", "sa"), None),
            P(),
            P(),
            P("sa", None),
            P("sa", None),
        ),
        out_specs=P(("grp", "sa"), None),
        check_vma=False,
    )
```

```python
import functools

import jax
import jax.numpy as jnp
import numpy as np
from jax import lax
from jax.experimental import pallas as pl
from jax.experimental.pallas import tpu as pltpu
from jax.sharding import PartitionSpec as P

LANES = 128
EPSILON = 1e-06
LINK = jnp.float16
FILTER_LINK = jnp.bfloat16
CONV_SCALE = 0.125


def rms_scale(values):
    return values * lax.rsqrt(jnp.mean(values * values, axis=-1, keepdims=True) + EPSILON)


def angles(first, second, period):
    product = np.outer(np.arange(first, dtype=np.int64), np.arange(second, dtype=np.int64)) % period
    phase = product.astype(np.float64) * (2 * np.pi / period)
    return np.cos(phase), np.sin(phase)


def contract(pattern, left, right):
    return jnp.einsum(
        pattern, left, right, precision=lax.Precision.HIGH, preferred_element_type=jnp.float32
    )


def remote(source, target, send, recv, where):
    return pltpu.make_async_remote_copy(
        src_ref=source,
        dst_ref=target,
        send_sem=send,
        recv_sem=recv,
        device_id=where,
        device_id_type=pl.DeviceIdType.MESH,
    )


def greet(shards, groups):
    me = lax.axis_index("sa")
    barrier = pltpu.get_barrier_semaphore()

    @pl.loop(1, shards)
    def _(step):
        pl.semaphore_signal(
            barrier,
            inc=1,
            device_id={"sa": lax.rem(me + step, shards)},
            device_id_type=pl.DeviceIdType.MESH,
        )

    for step in range(1, groups):
        pl.semaphore_signal(
            barrier,
            inc=1,
            device_id={"grp": lax.rem(lax.axis_index("grp") + step, groups)},
            device_id_type=pl.DeviceIdType.MESH,
        )
    pl.semaphore_wait(barrier, shards + groups - 2)


def scatter_copy(shards, number, step, source, target, send, recv):
    me = lax.axis_index("sa")
    to = lax.rem(me + step, shards)
    return remote(
        source.at[to], target.at[me], send.at[number, step], recv.at[number, step], {"sa": to}
    )


def start_scatter(shards, number, source, target, send, recv, local):
    me = lax.axis_index("sa")
    pltpu.make_async_copy(source.at[me], target.at[me], local.at[number]).start()

    @pl.loop(1, shards)
    def _(step):
        scatter_copy(shards, number, step, source, target, send, recv).start()


def finish_scatter(shards, number, source, target, send, recv, local):
    me = lax.axis_index("sa")

    @pl.loop(1, shards)
    def _(step):
        origin = lax.rem(me - step + shards, shards)
        remote(
            source.at[lax.rem(me + step, shards)],
            target.at[origin],
            send.at[number, step],
            recv.at[number, step],
            {"sa": lax.rem(me + step, shards)},
        ).wait()

    pltpu.make_async_copy(source.at[me], target.at[me], local.at[number]).wait()


def exchange_kernel(
    shards, groups, outer, inner, *refs
):
    sources, weights, targets, tables = refs[:2], refs[2:4], refs[4:6], refs[6:8]
    send, recv, local, own, z_send, z_recv, x_send, x_recv, y_send, y_recv, c_send, c_recv = refs[8:]
    me = lax.axis_index("sa")
    group = lax.axis_index("grp")
    core = lax.rem(me, 2)
    mid = lax.rem(me // 2, inner)
    far = me // (2 * inner)
    place = lambda o, m, c: (o * inner + m) * 2 + c

    def share(array, index):
        width = array.shape[-1] // groups
        return pl.ds(pl.multiple_of(index * width, 128), width)

    def z_copy(a, o_to, o_own):
        slot = place(o_own, mid, core)
        part = share(tables[a], group)
        return remote(
            weights[a].at[:, part],
            tables[a].at[slot, :, part],
            z_send.at[a, o_to],
            z_recv.at[a, o_own],
            {"sa": place(o_to, mid, core)},
        )

    def x_copy(a, o_own, index):
        slot = place(o_own, mid, core)
        part = tables[a].at[slot, :, share(tables[a], index)]
        other = lax.rem(group + 1, groups)
        return remote(part, part, x_send.at[a, o_own], x_recv.at[a, o_own], {"grp": other})

    def y_copy(a, o_own, step, m_own):
        slot = place(o_own, m_own, core)
        to = place(far, lax.rem(mid + step, inner), core)
        entry = tables[a].at[slot]
        return remote(entry, entry, y_send.at[a, step, o_own], y_recv.at[a, slot], {"sa": to})

    def c_copy(a, o_own, m_own, c_own):
        slot = place(o_own, m_own, c_own)
        row = o_own * inner + m_own
        entry = tables[a].at[slot]
        return remote(
            entry, entry, c_send.at[a, row], c_recv.at[a, row], {"sa": place(far, mid, 1 - core)}
        )

    def forward_y(a, o_own):
        @pl.loop(1, inner)
        def _(step):
            y_copy(a, o_own, step, mid).start()

        c_copy(a, o_own, mid, core).start()

    greet(shards, groups)
    for a in range(2):
        pltpu.make_async_copy(weights[a], tables[a].at[me], own.at[a]).start()

        @pl.loop(1, outer)
        def _(step):
            z_copy(a, lax.rem(far + step, outer), far).start()

    for number in range(2):
        start_scatter(shards, number, sources[number], targets[number], send, recv, local)
    for a in range(2):
        pltpu.make_async_copy(weights[a], tables[a].at[me], own.at[a]).wait()
        forward_y(a, far)
    for a in range(2):
        @pl.loop(1, outer)
        def _(step):
            origin = lax.rem(far - step + outer, outer)
            z_copy(a, far, origin).wait_recv()
            x_copy(a, origin, group).start()

    for a in range(2):
        @pl.loop(1, outer)
        def _(step):
            origin = lax.rem(far - step + outer, outer)
            x_copy(a, origin, lax.rem(group + 1, groups)).wait_recv()
            forward_y(a, origin)

    for a in range(2):
        @pl.loop(0, outer)
        def _(turn):
            origin = lax.rem(far - turn + outer, outer)

            @pl.loop(1, inner)
            def _(step):
                m_own = lax.rem(mid - step + inner, inner)
                y_copy(a, origin, step, m_own).wait_recv()
                c_copy(a, origin, m_own, core).start()

    for number in range(2):
        finish_scatter(shards, number, sources[number], targets[number], send, recv, local)
    for a in range(2):
        @pl.loop(0, outer)
        def _(o_own):
            @pl.loop(0, inner)
            def _(m_own):
                c_copy(a, o_own, m_own, 1 - core).wait_recv()
                c_copy(a, o_own, m_own, core).wait_send()

            @pl.loop(1, inner)
            def _(step):
                y_copy(a, o_own, step, mid).wait_send()

        @pl.loop(1, outer)
        def _(step):
            origin = lax.rem(far - step + outer, outer)
            x_copy(a, origin, group).wait_send()
            z_copy(a, lax.rem(far + step, outer), far).wait_send()


def anywhere(count):
    return [pl.BlockSpec(memory_space=pl.ANY)] * count


def exchange(packed, w_in, w_out):
    shards, groups = lax.axis_size("sa"), lax.axis_size("grp")
    inner = 1
    while inner * inner * 4 <= shards // 2:
        inner *= 2
    outer = shards // (2 * inner)
    dma = pltpu.SemaphoreType.DMA
    shapes = [jax.ShapeDtypeStruct(v.shape, v.dtype) for v in packed] + [
        jax.ShapeDtypeStruct((shards,) + w.shape, w.dtype) for w in (w_in, w_out)
    ]
    return pl.pallas_call(
        functools.partial(exchange_kernel, shards, groups, outer, inner),
        out_shape=shapes,
        in_specs=anywhere(4),
        out_specs=anywhere(4),
        scratch_shapes=[
            dma((2, shards)),
            dma((2, shards)),
            dma((2,)),
            dma((2,)),
            dma((2, outer)),
            dma((2, outer)),
            dma((2, outer)),
            dma((2, outer)),
            dma((2, inner, outer)),
            dma((2, shards)),
            dma((2, outer * inner)),
            dma((2, outer * inner)),
        ],
        compiler_params=pltpu.CompilerParams(collective_id=1, has_side_effects=True),
    )(*packed, w_in, w_out)


def on_device(tokens, kernel_re, kernel_im, mix_gain, mlp_gain, w_in, w_out):
    shards = lax.axis_size("sa")
    rows, channels = tokens.shape
    part = channels // shards
    blocks = rows // LANES
    total = shards * rows
    outer = total // LANES

    def pack(values, link):
        return values.astype(link).reshape(blocks, LANES, shards, part).transpose(2, 0, 3, 1)

    normed = rms_scale(tokens) * mix_gain
    signal = lax.all_to_all(pack(normed, LINK), "sa", split_axis=0, concat_axis=0, tiled=True)
    signal = signal.reshape(outer, part, LANES).astype(jnp.float32)
    *moved, w_in, w_out = exchange(
        [pack(kernel_re, FILTER_LINK), pack(kernel_im, FILTER_LINK)], w_in, w_out
    )
    moved = [values.reshape(outer, part, LANES) for values in moved]
    w_in = w_in.reshape(channels, -1)
    w_out = w_out.reshape(-1, channels)

    def by_frequency(values):
        ordered = values.transpose(1, 0, 2).reshape(part, LANES, outer)
        return ordered.transpose(2, 0, 1).astype(jnp.float32)

    filter_re = by_frequency(moved[0])
    filter_im = by_frequency(moved[1])

    cos_outer, sin_outer = angles(outer, outer, outer)
    cos_inner, sin_inner = angles(LANES, LANES, LANES)
    cos_twist, sin_twist = angles(outer, LANES, total)
    first = jnp.asarray(np.concatenate([cos_outer, -sin_outer], 0), jnp.float32)
    last = jnp.asarray(np.concatenate([cos_outer, -sin_outer], 1), jnp.float32)
    forward = jnp.asarray(
        np.block([[cos_inner, -sin_inner], [sin_inner, cos_inner]]), jnp.float32
    )
    backward = jnp.asarray(
        np.block([[cos_inner, sin_inner], [-sin_inner, cos_inner]]), jnp.float32
    )
    cos_twist = jnp.asarray(cos_twist[:, None, :], jnp.float32)
    sin_twist = jnp.asarray(sin_twist[:, None, :], jnp.float32)

    mid = contract("ca,adb->cdb", first, signal)
    mid_re, mid_im = mid[:outer], mid[outer:]
    turned = jnp.concatenate(
        [mid_re * cos_twist + mid_im * sin_twist, mid_im * cos_twist - mid_re * sin_twist], -1
    )
    spectrum = contract("cdb,be->cde", turned, forward)
    spec_re, spec_im = spectrum[..., :LANES], spectrum[..., LANES:]
    filtered = jnp.concatenate(
        [spec_re * filter_re - spec_im * filter_im, spec_re * filter_im + spec_im * filter_re], -1
    )
    back = contract("cde,eb->cdb", filtered, backward)
    back_re, back_im = back[..., :LANES], back[..., LANES:]
    untwisted = jnp.concatenate(
        [back_re * cos_twist - back_im * sin_twist, back_im * cos_twist + back_re * sin_twist], 0
    )
    conv = contract("ac,cdb->adb", last, untwisted)
    conv = (conv * (CONV_SCALE / total)).astype(LINK).reshape(shards, blocks, part, LANES)
    conv = lax.all_to_all(conv, "sa", split_axis=0, concat_axis=0, tiled=True)
    conv = conv.transpose(1, 3, 0, 2).reshape(rows, channels).astype(jnp.float32) * (1 / CONV_SCALE)

    mixed = tokens + conv * jax.nn.sigmoid(normed)
    scaled = (rms_scale(mixed) * mlp_gain).astype(jnp.bfloat16)
    hidden_pre = jnp.dot(
        scaled, w_in, preferred_element_type=jnp.float32
    )
    hidden = jax.nn.gelu(hidden_pre, approximate=True).astype(jnp.bfloat16)
    branch = jnp.dot(
        hidden, w_out, preferred_element_type=jnp.float32
    )
    return mixed + branch


def solution(mesh):
    return jax.shard_map(
        on_device,
        mesh=mesh,
        in_specs=(
            P(("grp", "sa"), None),
            P(("grp", "sa"), None),
            P(("grp", "sa"), None),
            P(),
            P(),
            P("sa", None),
            P("sa", None),
        ),
        out_specs=P(("grp", "sa"), None),
        check_vma=False,
    )
```

```python
import jax
import jax.numpy as jnp
import numpy as np
from jax import lax
from jax.sharding import PartitionSpec as P

LANES = 128
EPSILON = 1e-06
LINK = jnp.float16
CONV_SCALE = 0.125


def rms_scale(values):
    return values * lax.rsqrt(jnp.mean(values * values, axis=-1, keepdims=True) + EPSILON)


def angles(first, second, period):
    product = np.outer(np.arange(first, dtype=np.int64), np.arange(second, dtype=np.int64)) % period
    phase = product.astype(np.float64) * (2 * np.pi / period)
    return np.cos(phase), np.sin(phase)


def contract(pattern, left, right):
    return jnp.einsum(
        pattern, left, right, precision=lax.Precision.HIGH, preferred_element_type=jnp.float32
    )


def half_of(weights, group):
    width = weights.shape[1] // 2
    return jnp.where(group == 0, weights[:, :width], weights[:, width:])


def join(mine, other, group):
    left = jnp.where(group == 0, mine, other)
    return jnp.concatenate([left, jnp.where(group == 0, other, mine)], 1)


def on_device(tokens, kernel_re, kernel_im, mix_gain, mlp_gain, w_in, w_out):
    shards = lax.axis_size("sa")
    rows, channels = tokens.shape
    part = channels // shards
    blocks = rows // LANES
    total = shards * rows
    outer = total // LANES

    def pack(values):
        return values.astype(LINK).reshape(blocks, LANES, shards, part).transpose(2, 0, 3, 1)

    def to_channels(packed):
        moved = lax.all_to_all(packed, "sa", split_axis=0, concat_axis=0, tiled=True)
        return moved.reshape(outer, part, LANES)

    group = lax.axis_index("grp")
    swap = [(0, 1), (1, 0)]
    in_mine = lax.all_gather(half_of(w_in, group), "sa", axis=0, tiled=True)
    packed_im, out_half, in_mine = lax.optimization_barrier(
        (pack(kernel_im), half_of(w_out, group), in_mine)
    )
    in_other = lax.ppermute(in_mine, "grp", swap)
    out_mine = lax.all_gather(out_half, "sa", axis=0, tiled=True)

    normed = rms_scale(tokens) * mix_gain
    packed_re = pack(kernel_re)
    moved_re = to_channels(packed_re)
    packed_normed, out_mine = lax.optimization_barrier((pack(normed), out_mine))
    out_other = lax.ppermute(out_mine, "grp", swap)
    signal = to_channels(packed_normed).astype(jnp.float32)

    def by_frequency(moved):
        ordered = moved.transpose(1, 0, 2).reshape(part, LANES, outer)
        return ordered.transpose(2, 0, 1).astype(jnp.float32)

    filter_re = by_frequency(moved_re)
    filter_im = by_frequency(to_channels(packed_im))

    cos_outer, sin_outer = angles(outer, outer, outer)
    cos_inner, sin_inner = angles(LANES, LANES, LANES)
    cos_twist, sin_twist = angles(outer, LANES, total)
    first = jnp.asarray(np.concatenate([cos_outer, -sin_outer], 0), jnp.float32)
    last = jnp.asarray(np.concatenate([cos_outer, -sin_outer], 1), jnp.float32)
    forward = jnp.asarray(
        np.block([[cos_inner, -sin_inner], [sin_inner, cos_inner]]), jnp.float32
    )
    backward = jnp.asarray(
        np.block([[cos_inner, sin_inner], [-sin_inner, cos_inner]]), jnp.float32
    )
    cos_twist = jnp.asarray(cos_twist[:, None, :], jnp.float32)
    sin_twist = jnp.asarray(sin_twist[:, None, :], jnp.float32)

    mid = contract("ca,adb->cdb", first, signal)
    mid_re, mid_im = mid[:outer], mid[outer:]
    turned = jnp.concatenate(
        [mid_re * cos_twist + mid_im * sin_twist, mid_im * cos_twist - mid_re * sin_twist], -1
    )
    spectrum = contract("cdb,be->cde", turned, forward)
    spec_re, spec_im = spectrum[..., :LANES], spectrum[..., LANES:]
    filtered = jnp.concatenate(
        [spec_re * filter_re - spec_im * filter_im, spec_re * filter_im + spec_im * filter_re], -1
    )
    back = contract("cde,eb->cdb", filtered, backward)
    back_re, back_im = back[..., :LANES], back[..., LANES:]
    untwisted = jnp.concatenate(
        [back_re * cos_twist - back_im * sin_twist, back_im * cos_twist + back_re * sin_twist], 0
    )
    conv = contract("ac,cdb->adb", last, untwisted)
    conv = (conv * (CONV_SCALE / total)).astype(LINK).reshape(shards, blocks, part, LANES)
    conv, in_other = lax.optimization_barrier((conv, in_other))
    conv = lax.all_to_all(conv, "sa", split_axis=0, concat_axis=0, tiled=True)
    conv = conv.transpose(1, 3, 0, 2).reshape(rows, channels).astype(jnp.float32) * (1 / CONV_SCALE)

    mixed = tokens + conv * jax.nn.sigmoid(normed)
    scaled = (rms_scale(mixed) * mlp_gain).astype(jnp.bfloat16)
    hidden_pre = jnp.dot(
        scaled, join(in_mine, in_other, group), preferred_element_type=jnp.float32
    )
    hidden = jax.nn.gelu(hidden_pre, approximate=True).astype(jnp.bfloat16)
    branch = jnp.dot(
        hidden, join(out_mine, out_other, group), preferred_element_type=jnp.float32
    )
    return mixed + branch


def solution(mesh):
    return jax.shard_map(
        on_device,
        mesh=mesh,
        in_specs=(
            P(("grp", "sa"), None),
            P(("grp", "sa"), None),
            P(("grp", "sa"), None),
            P(),
            P(),
            P("sa", None),
            P("sa", None),
        ),
        out_specs=P(("grp", "sa"), None),
        check_vma=False,
    )
```
